128 devices in a mesh: dp: 32 (over z, x, core), tensor: 4 (over y).
Axes of the slice: x: 4, y: 4, z: 4, core: 2. Of those that a mesh axis runs over, the one named last changes fastest.
Arguments:
- tokens: bfloat16 [16384, 1152], P(('dp', 'tensor')), may hold values from -6 to 6
- document_ids: int32 [16384], P('dp'), may hold values from -1 to 127, as said below
- cotangent: bfloat16 [16384, 1152], P(('dp', 'tensor')), may hold values from -6 to 6
- query_weight: float32 [1152, 1024], P('dp', 'tensor'), may hold values from -0.1875 to 0.1875
- keyvalue_weight: float32 [1152, 512], P('dp'), may hold values from -0.1875 to 0.1875
- output_weight: float32 [1024, 1152], P('tensor', 'dp'), may hold values from -0.1875 to 0.1875
- gate_weight: float32 [1152, 6912], P('dp', 'tensor'), may hold values from -0.1875 to 0.1875
- up_weight: float32 [1152, 6912], P('dp', 'tensor'), may hold values from -0.1875 to 0.1875
- down_weight: float32 [6912, 1152], P('tensor', 'dp'), may hold values from -0.078125 to 0.078125
- norm_gains: float32 [5120], P('dp'), may hold values from 0.5 to 1.5
- query_first: float32 [1152, 1024], P('dp', 'tensor'), may hold values from -80 to 80
- query_second: float32 [1152, 1024], P('dp', 'tensor'), may hold values from 425.984 to 6881.28
- keyvalue_first: float32 [1152, 512], P('dp'), may hold values from -80 to 80
- keyvalue_second: float32 [1152, 512], P('dp'), may hold values from 425.984 to 6881.28
- output_first: float32 [1024, 1152], P('tensor', 'dp'), may hold values from -80 to 80
- output_second: float32 [1024, 1152], P('tensor', 'dp'), may hold values from 425.984 to 6881.28
- gate_first: float32 [1152, 6912], P('dp', 'tensor'), may hold values from -40 to 40
- gate_second: float32 [1152, 6912], P('dp', 'tensor'), may hold values from 108.1344 to 1720.32
- up_first: float32 [1152, 6912], P('dp', 'tensor'), may hold values from -40 to 40
- up_second: float32 [1152, 6912], P('dp', 'tensor'), may hold values from 108.1344 to 1720.32
- down_first: float32 [6912, 1152], P('tensor', 'dp'), may hold values from -80 to 80
- down_second: float32 [6912, 1152], P('tensor', 'dp'), may hold values from 425.984 to 6881.28
- gain_first: float32 [5120], P('dp'), may hold values from -80 to 80
- gain_second: float32 [5120], P('dp'), may hold values from 425.984 to 6881.28
Outputs:
- block_output: bfloat16 [16384, 1152], P(('dp', 'tensor'))
- token_grad: bfloat16 [16384, 1152], P(('dp', 'tensor'))
- query_first_next: float32 [1152, 1024], P('dp', 'tensor')
- query_second_next: float32 [1152, 1024], P('dp', 'tensor')
- query_weight_next: float32 [1152, 1024], P('dp', 'tensor')
- keyvalue_first_next: float32 [1152, 512], P('dp')
- keyvalue_second_next: float32 [1152, 512], P('dp')
- keyvalue_weight_next: float32 [1152, 512], P('dp')
- output_first_next: float32 [1024, 1152], P('tensor', 'dp')
- output_second_next: float32 [1024, 1152], P('tensor', 'dp')
- output_weight_next: float32 [1024, 1152], P('tensor', 'dp')
- gate_first_next: float32 [1152, 6912], P('dp', 'tensor')
- gate_second_next: float32 [1152, 6912], P('dp', 'tensor')
- gate_weight_next: float32 [1152, 6912], P('dp', 'tensor')
- up_first_next: float32 [1152, 6912], P('dp', 'tensor')
- up_second_next: float32 [1152, 6912], P('dp', 'tensor')
- up_weight_next: float32 [1152, 6912], P('dp', 'tensor')
- down_first_next: float32 [6912, 1152], P('tensor', 'dp')
- down_second_next: float32 [6912, 1152], P('tensor', 'dp')
- down_weight_next: float32 [6912, 1152], P('tensor', 'dp')
- gain_first_next: float32 [5120], P('dp')
- gain_second_next: float32 [5120], P('dp')
- norm_gains_next: float32 [5120], P('dp')
The draws below stay inside these ranges and needn't reach their ends.
Inputs may be any that keep to these rules, and one draw needn't show every extreme that they name: `document_ids`: each pack of 512 tokens starts with document 0, which is longer than 384 tokens; ids never fall within a pack and count up by one from document to document; a pack's last positions, at most 64 of them, may be padding (-1); in every draw some pack is a single document of 512 tokens, and some pack ends in documents of one token each.
All inputs are finite; a program needn't handle non-finite values.
Results may differ from the reference program's by a relative error of at most 0.035.
Values may be sent and summed in bfloat16 or wider, within the bound.
A program may use at most 128 MiB of HBM per device.

```python
import math
import jax
import jax.numpy as jnp
from jax import lax

D = 1152
H = 4
HD = 256
FF = 6912
STEP = 10
PACK = 512
TOKENS = 16384
GAINS = 5120


def draw_document_ids(key, part):
    key = jax.random.fold_in(key, 7)
    group_total = TOKENS // PACK
    live_key, first_key, cut_key, full_key = jax.random.split(key, 4)
    group_index = jnp.arange(group_total, dtype=jnp.int32)
    full_group = jax.random.randint(full_key, (), 0, group_total)
    split_group = (full_group + 1) % group_total
    shortfall = jax.random.randint(live_key, (group_total,), 0, PACK // 8 + 1)
    shortfall = jnp.where((group_index == full_group) | (group_index == split_group), 0, shortfall)
    live_count = PACK - shortfall
    first_length = jax.random.randint(first_key, (group_total,), 3 * PACK // 4 + 1, PACK + 1)
    first_length = jnp.minimum(first_length, live_count)
    first_length = jnp.where(group_index == full_group, PACK, first_length)
    first_length = jnp.where(group_index == split_group, 3 * PACK // 4 + 1, first_length)
    position = jnp.arange(PACK, dtype=jnp.int32)[None, :]
    random_marks = jax.random.randint(cut_key, (group_total, PACK), 0, 48) == 0
    random_marks = random_marks | (group_index == split_group)[:, None]
    cut_marks = random_marks & (position > first_length[:, None])
    later_ids = 1 + jnp.cumsum(cut_marks.astype(jnp.int32), axis=1)
    segment_ids = jnp.where(position < first_length[:, None], 0, later_ids)
    segment_ids = jnp.where(position >= live_count[:, None], -1, segment_ids)
    return segment_ids.reshape(TOKENS).astype(jnp.int32)


def level_of(own_key, dims, shards, low, top_value):
    def one(dim, blocks):
        draws = jax.random.uniform(jax.random.fold_in(jax.random.fold_in(own_key, 6), dim), (blocks,), jnp.float32, low / len(shards), top_value / len(shards))
        return jnp.repeat(jnp.exp(draws), dims[dim] // blocks).reshape((-1,) + (1,) * (len(dims) - dim - 1))

    factor_of = one(*shards[0])
    for cut in shards[1:]:
        factor_of = factor_of * one(*cut)
    return factor_of


def bell_draw(key, shape, deviation, most, cuts=(), held_as=jnp.bfloat16):
    drawn = deviation * jax.random.normal(key, shape, jnp.float32)
    if cuts:
        drawn = drawn * level_of(key, shape, cuts, -0.22, 0.18)
    return jnp.clip(drawn, -most, most).astype(held_as)


def setup_inputs(seed: int = 0) -> dict:
    streams_of = jax.random.split(jax.random.key(seed), 25)
    return {
        "tokens": bell_draw(streams_of[0], (TOKENS, D), 1.0, 6.0, ((0, 128),)),
        "document_ids": draw_document_ids(jax.random.fold_in(streams_of[24], 71), 0),
        "cotangent": bell_draw(streams_of[2], (TOKENS, D), 1.0, 6.0, ((0, 128),)),
        "query_weight": bell_draw(streams_of[3], (D, H * HD), D ** -0.5, 0.1875, ((0, 32), (1, 4)), jnp.float32),
        "keyvalue_weight": bell_draw(streams_of[4], (D, 2 * HD), D ** -0.5, 0.1875, ((0, 32),), jnp.float32),
        "output_weight": bell_draw(streams_of[5], (H * HD, D), (H * HD) ** -0.5, 0.1875, ((0, 4), (1, 32)), jnp.float32),
        "gate_weight": bell_draw(streams_of[6], (D, FF), D ** -0.5, 0.1875, ((0, 32), (1, 4)), jnp.float32),
        "up_weight": bell_draw(streams_of[7], (D, FF), D ** -0.5, 0.1875, ((0, 32), (1, 4)), jnp.float32),
        "down_weight": bell_draw(streams_of[8], (FF, D), FF ** -0.5, 0.078125, ((0, 4), (1, 32)), jnp.float32),
        "norm_gains": jnp.clip(1.0 + 0.1 * jax.random.normal(streams_of[9], (GAINS,), jnp.float32), 0.5, 1.5),
        "query_first": bell_draw(streams_of[10], (D, H * HD), (0.11 * TOKENS ** 0.5), 80.0, ((0, 32), (1, 4)), jnp.float32),
        "query_second": jnp.clip(jnp.exp(math.log(6881.28) - 2.7821581 * jax.random.uniform(streams_of[11], (D, H * HD), jnp.float32) ** level_of(streams_of[11], (D, H * HD), ((0, 32), (1, 4)), -0.2, 0.2)), 425.984, 6881.28),
        "keyvalue_first": bell_draw(streams_of[12], (D, 2 * HD), (0.11 * TOKENS ** 0.5), 80.0, ((0, 32),), jnp.float32),
        "keyvalue_second": jnp.clip(jnp.exp(math.log(6881.28) - 2.7821581 * jax.random.uniform(streams_of[13], (D, 2 * HD), jnp.float32) ** level_of(streams_of[13], (D, 2 * HD), ((0, 32),), -0.2, 0.2)), 425.984, 6881.28),
        "output_first": bell_draw(streams_of[14], (H * HD, D), (0.11 * TOKENS ** 0.5), 80.0, ((0, 4), (1, 32)), jnp.float32),
        "output_second": jnp.clip(jnp.exp(math.log(6881.28) - 2.7821581 * jax.random.uniform(streams_of[15], (H * HD, D), jnp.float32) ** level_of(streams_of[15], (H * HD, D), ((0, 4), (1, 32)), -0.2, 0.2)), 425.984, 6881.28),
        "gate_first": bell_draw(streams_of[16], (D, FF), (0.055 * TOKENS ** 0.5), 40.0, ((0, 32), (1, 4)), jnp.float32),
        "gate_second": jnp.clip(jnp.exp(math.log(1720.32) - 2.7668907 * jax.random.uniform(streams_of[17], (D, FF), jnp.float32) ** level_of(streams_of[17], (D, FF), ((0, 32), (1, 4)), -0.2, 0.2)), 108.1344, 1720.32),
        "up_first": bell_draw(streams_of[18], (D, FF), (0.055 * TOKENS ** 0.5), 40.0, ((0, 32), (1, 4)), jnp.float32),
        "up_second": jnp.clip(jnp.exp(math.log(1720.32) - 2.7668907 * jax.random.uniform(streams_of[19], (D, FF), jnp.float32) ** level_of(streams_of[19], (D, FF), ((0, 32), (1, 4)), -0.2, 0.2)), 108.1344, 1720.32),
        "down_first": bell_draw(streams_of[20], (FF, D), (0.11 * TOKENS ** 0.5), 80.0, ((0, 4), (1, 32)), jnp.float32),
        "down_second": jnp.clip(jnp.exp(math.log(6881.28) - 2.7821581 * jax.random.uniform(streams_of[21], (FF, D), jnp.float32) ** level_of(streams_of[21], (FF, D), ((0, 4), (1, 32)), -0.2, 0.2)), 425.984, 6881.28),
        "gain_first": bell_draw(streams_of[22], (GAINS,), (0.11 * TOKENS ** 0.5), 80.0, ((0, 32),), jnp.float32),
        "gain_second": jnp.clip(jnp.exp(math.log(6881.28) - 2.7821581 * jax.random.uniform(streams_of[23], (GAINS,), jnp.float32) ** level_of(streams_of[23], (GAINS,), ((0, 32),), -0.2, 0.2)), 425.984, 6881.28),
    }


@jax.custom_vjp
def low(v):
    return lax.optimization_barrier(v.astype(jnp.bfloat16)).astype(jnp.float32)

@jax.custom_vjp
def low_back(v):
    return v

def low_keep(v):
    return (low(v), None)

def low_pass(kept, grad):
    return (grad,)

def back_keep(v):
    return (v, None)

def back_low(kept, grad):
    return (low(grad),)
low.defvjp(low_keep, low_pass)
low_back.defvjp(back_keep, back_low)
norm_epsilon = 1e-06
rope_base = 1000000.0
beta_first = 0.9
beta_second = 0.95
adam_epsilon = 1e-08
weight_decay = 0.1
matrix_rate = 2.0
gain_rate = 1.0
highest = lax.Precision.HIGHEST

def root_norm(values, gain):
    return values * lax.rsqrt(lax.optimization_barrier(jnp.mean(values * values, axis=-1, keepdims=True)) + norm_epsilon) * gain

def document_positions(document_ids):
    length = document_ids.shape[0]
    index = jnp.arange(length, dtype=jnp.int32)
    changed = jnp.concatenate([jnp.ones((1,), dtype=bool), document_ids[1:] != document_ids[:-1]])
    starts = lax.cummax(jnp.where(changed, index, jnp.zeros_like(index)), axis=0)
    return index - starts

def rope_tables(positions, width):
    half_width = width // 2
    exponent = jnp.arange(half_width, dtype=jnp.float32) * (2.0 / width)
    frequency = rope_base ** (-exponent)
    angle_table = positions.astype(jnp.float32)[:, None] * frequency[None, :]
    return (jnp.cos(angle_table), jnp.sin(angle_table))

def rotate(values, cosine_part, sine_part):
    half_width = values.shape[-1] // 2
    former = values[..., :half_width]
    latter = values[..., half_width:]
    return jnp.concatenate([former * cosine_part - latter * sine_part, latter * cosine_part + former * sine_part], axis=-1)

def allowed_mask(document_ids):
    length = document_ids.shape[0]
    index = jnp.arange(length, dtype=jnp.int32)
    same = (document_ids[:, None] == document_ids[None, :]) & (document_ids[:, None] >= 0) & (index[None, :] <= index[:, None])
    return same | (index[None, :] == index[:, None])

def adam_update(weight, gradient, first, second, rate, decay_rate):
    first_new = beta_first * first + (1.0 - beta_first) * gradient
    second_new = beta_second * second + (1.0 - beta_second) * gradient * gradient
    first_hat = first_new / (1.0 - beta_first ** STEP)
    second_hat = second_new / (1.0 - beta_second ** STEP)
    weight_new = weight - rate * (first_hat / (jnp.sqrt(second_hat) + adam_epsilon) + decay_rate * weight)
    return (first_new, second_new, weight_new)

def group_forward(inputs, document_ids, gain_values, query_full, keyvalue_full, output_full, gate_full, up_full, down_full):
    pre_attn = gain_values[0:D]
    post_attn = gain_values[D:2 * D]
    pre_ffn = gain_values[2 * D:3 * D]
    post_ffn = gain_values[3 * D:4 * D]
    query_gain = gain_values[4 * D:4 * D + HD]
    key_gain = gain_values[4 * D + HD:4 * D + 2 * HD]
    cosine_part, sine_part = rope_tables(document_positions(document_ids), HD)
    normed = low(root_norm(inputs, pre_attn))
    query_raw = low_back(jnp.dot(normed, query_full, precision=highest))
    query_heads = jnp.transpose(query_raw.reshape(PACK, H, HD), (1, 0, 2))
    query_rot = low(rotate(root_norm(query_heads, query_gain), cosine_part, sine_part))
    keyvalue_raw = jnp.dot(normed, keyvalue_full, precision=highest)
    key_rot = low(rotate(root_norm(low_back(keyvalue_raw[:, :HD]), key_gain), cosine_part, sine_part))
    value_low = low_back(low(keyvalue_raw[:, HD:]))
    scores = low_back(jnp.einsum('hqd,kd->hqk', query_rot, key_rot, precision=highest) * HD ** (-0.5))
    scores = jnp.where(allowed_mask(document_ids)[None], scores, -1e+30)
    probabilities = low(jax.nn.softmax(scores, axis=-1))
    heads = low_back(low(jnp.einsum('hqk,kd->hqd', probabilities, value_low, precision=highest)))
    merged = jnp.transpose(heads, (1, 0, 2)).reshape(PACK, H * HD)
    attention = low_back(jnp.dot(merged, output_full, precision=highest))
    middle = inputs + root_norm(attention, post_attn)
    ffn_normed = low(root_norm(middle, pre_ffn))
    gate_values = low_back(jnp.dot(ffn_normed, gate_full, precision=highest))
    up_values = low_back(jnp.dot(ffn_normed, up_full, precision=highest))
    hidden = low(jax.nn.gelu(gate_values, approximate=True) * up_values)
    ffn_out = low_back(jnp.dot(hidden, down_full, precision=highest))
    return middle + root_norm(ffn_out, post_ffn)

def reference(tokens, document_ids, cotangent, query_weight, keyvalue_weight, output_weight, gate_weight, up_weight, down_weight, norm_gains, query_first, query_second, keyvalue_first, keyvalue_second, output_first, output_second, gate_first, gate_second, up_first, up_second, down_first, down_second, gain_first, gain_second):
    group_docs = document_ids.reshape(-1, PACK)
    live = (document_ids >= 0).astype(jnp.float32)[:, None]

    def forward(inputs, gain_values, query_w, keyvalue_w, output_w, gate_w, up_w, down_w):
        gain_low = low(gain_values)
        query_low = low(query_w)
        keyvalue_low = low(keyvalue_w)
        output_low = low(output_w)
        gate_low = low(gate_w)
        up_low = low(up_w)
        down_low = low(down_w)

        def one_group(pair):
            return group_forward(pair[0], pair[1], gain_low, query_low, keyvalue_low, output_low, gate_low, up_low, down_low)
        grouped = lax.map(jax.checkpoint(one_group), (inputs.reshape(-1, PACK, D), group_docs))
        return grouped.reshape(-1, D)
    primal = (tokens.astype(jnp.float32), norm_gains, query_weight, keyvalue_weight, output_weight, gate_weight, up_weight, down_weight)
    output_values, pullback = jax.vjp(forward, *primal)
    gradients = pullback(cotangent.astype(jnp.float32) * live)
    token_grad = gradients[0].astype(jnp.bfloat16)
    gain_grad = gradients[1]
    query_next = adam_update(query_weight, gradients[2], query_first, query_second, matrix_rate * D ** (-0.5), weight_decay)
    keyvalue_next = adam_update(keyvalue_weight, gradients[3], keyvalue_first, keyvalue_second, matrix_rate * D ** (-0.5), weight_decay)
    output_next = adam_update(output_weight, gradients[4], output_first, output_second, matrix_rate * (H * HD) ** (-0.5), weight_decay)
    gate_next = adam_update(gate_weight, gradients[5], gate_first, gate_second, matrix_rate * D ** (-0.5), weight_decay)
    up_next = adam_update(up_weight, gradients[6], up_first, up_second, matrix_rate * D ** (-0.5), weight_decay)
    down_next = adam_update(down_weight, gradients[7], down_first, down_second, matrix_rate * FF ** (-0.5), weight_decay)
    gain_next = adam_update(norm_gains, gain_grad, gain_first, gain_second, gain_rate, 0.0)
    return (output_values.astype(jnp.bfloat16), token_grad, query_next[0], query_next[1], query_next[2], keyvalue_next[0], keyvalue_next[1], keyvalue_next[2], output_next[0], output_next[1], output_next[2], gate_next[0], gate_next[1], gate_next[2], up_next[0], up_next[1], up_next[2], down_next[0], down_next[1], down_next[2], gain_next[0], gain_next[1], gain_next[2])
```

```python
import functools

import jax
import jax.numpy as jnp
import numpy as np
from jax import lax
from jax.experimental import pallas as pl
from jax.experimental.pallas import tpu as pltpu
from jax.sharding import PartitionSpec as P

D = 1152
H = 4
HD = 256
FF = 6912
STEP = 10


norm_epsilon = 1e-06
rope_base = 1000000.0
beta_first = 0.9
beta_second = 0.95
adam_epsilon = 1e-08
weight_decay = 0.1
matrix_rate = 2.0
gain_rate = 1.0


def adam_update(weight, gradient, first, second, rate, decay_rate):
    first_new = beta_first * first + (1.0 - beta_first) * gradient
    second_new = beta_second * second + (1.0 - beta_second) * gradient * gradient
    first_hat = first_new / (1.0 - beta_first**STEP)
    second_hat = second_new / (1.0 - beta_second**STEP)
    weight_new = weight - rate * (
        first_hat / (jnp.sqrt(second_hat) + adam_epsilon) + decay_rate * weight
    )
    return (first_new, second_new, weight_new)


FP = 1792
QKVO, FFN, QKVO_REST, FFN_REST, DOWN = range(5)
GATE_UP = FFN
WIDTHS = (1024, 3 * FP, 1152, 3 * FP)
LEAD = (2, 2, 4, 4, 16)
REST_LEAD = (2, 4, 16)
SAVED = (
    (LEAD + (WIDTHS[QKVO],), jnp.bfloat16),
    (REST_LEAD + (WIDTHS[QKVO_REST],), jnp.bfloat16),
    ((4, 128, D), jnp.bfloat16),
    ((512, HD), jnp.float32),
    ((512, HD), jnp.float32),
    ((512, HD), jnp.bfloat16),
    ((512, HD), jnp.bfloat16),
    ((512, HD), jnp.bfloat16),
    ((512, 512), jnp.float32),
    ((4, 128, HD), jnp.bfloat16),
    ((4, 128, D), jnp.bfloat16),
    ((512, HD // 2), jnp.float32),
    ((512, HD // 2), jnp.float32),
)
MESH = pl.DeviceIdType.MESH
LOW = jnp.bfloat16
F32 = jnp.float32
VMEM_LIMIT = 58 * 1024 * 1024


def order_row():
    p = lax.broadcasted_iota(jnp.int32, (1, D), 1)
    rest = p >= 1024
    a = jnp.where(rest, (p >> 4) & 3, (p >> 6) & 3)
    b = jnp.where(rest, (p >> 2) & 3, (p >> 4) & 3)
    c = jnp.where(rest, (p >> 6) & 1, (p >> 8) & 1)
    second = (p >= 512) & (p < 1024)
    z, x = jnp.where(second, b, a), jnp.where(second, a, b)
    row = jnp.where(rest, 32 + (p & 3), (p & 15) + jnp.where(second, 16, 0))
    return ((z * 4 + x) * 2 + c) * 36 + row


def gain_row(n, order):
    p = lax.broadcasted_iota(jnp.int32, (1, D), 1)
    flat = n * D + (order if n < 4 else p)
    dp = jnp.floor((flat.astype(jnp.float32) + 0.5) * (1.0 / 160.0)).astype(jnp.int32)
    entry = flat - dp * 160
    spot = (dp & 1) * 16 + (dp >> 3) * 4 + ((dp >> 1) & 3)
    holder = spot * 4 + jnp.where(entry >= 128, 1, 0)
    if n == 4:
        holder = jnp.where(p < 2 * HD, holder, 128)
    return holder, entry & 127


def place():
    dp = lax.axis_index("dp")
    return dp // 8, (dp // 2) % 4, dp % 2, lax.axis_index("tensor")


def neighbour(h, z, x, c, y, ds, df, other=False):
    dz, dx = (ds, df) if h == 0 else (df, ds)
    core = 1 - c if other else c
    return ((((z + dz) % 4) * 4 + (x + dx) % 4) * 2 + core, y)


def along(y, step):
    return (lax.axis_index("dp"), (y + step) % 4)


def greet(z, x, c, y, planes, rings, far=False):
    devices = []
    if planes:
        for h, df, other in (
            (0, 1, False),
            (0, -1, False),
            (1, 1, False),
            (1, -1, False),
            (0, 0, True),
        ):
            devices.append(neighbour(h, z, x, c, y, 0, df, other))
    if rings:
        devices += [along(y, 1), along(y, 3)]
    if far:
        devices.append(along(y, 2))
    barrier = pltpu.get_barrier_semaphore()
    for device in devices:
        pl.semaphore_signal(barrier, inc=1, device_id=device, device_id_type=MESH)
    return lambda: pl.semaphore_wait(barrier, len(devices))


class Sender:
    def __init__(self, send, recv):
        self.send, self.recv, self.started = send, recv, []

    def push(self, at, source, target, device):
        copy = pltpu.make_async_remote_copy(
            src_ref=source,
            dst_ref=target,
            send_sem=self.send.at[at],
            recv_sem=self.recv.at[at],
            device_id=device,
            device_id_type=MESH,
        )
        copy.start()
        self.started.append(copy)
        return copy

    def close(self):
        for copy in self.started:
            copy.wait_send()


def split(width):
    return (width // 128 + 1) // 2 * 128


def nt(a, b):
    return lax.dot_general(a, b, (((1,), (1,)), ((), ())), preferred_element_type=F32)


def nn(a, b):
    return jnp.dot(a, b, preferred_element_type=F32)


def rms_scale(u):
    return lax.rsqrt(jnp.mean(u * u, axis=-1, keepdims=True) + norm_epsilon)


def rms_back(u, gain, e):
    r = rms_scale(u)
    unit = u * r
    scaled = e * gain
    inner = jnp.mean(scaled * unit, axis=-1, keepdims=True)
    return r * (scaled - unit * inner), jnp.sum(e * unit, axis=0, keepdims=True)


def turn(values, cosine, sine):
    former, latter = values[:, : HD // 2], values[:, HD // 2 :]
    return jnp.concatenate(
        [former * cosine - latter * sine, latter * cosine + former * sine], axis=1
    )


class RingGather:
    def __init__(self, sender, slot, y, full):
        self.sender, self.slot, self.y, self.full = sender, slot, y, full
        self.half = full.shape[1] // 2

    def start(self):
        block = self.full.at[self.y]
        self.from_left = self.sender.push((self.slot, 0), block, block, along(self.y, 1))
        self.from_right = self.sender.push((self.slot, 1), block, block, along(self.y, 3))

    def forward(self):
        self.from_left.wait_recv()
        part = self.full.at[(self.y + 3) % 4, pl.ds(0, self.half)]
        self.far_left = self.sender.push((self.slot, 2), part, part, along(self.y, 1))
        self.from_right.wait_recv()
        part = self.full.at[(self.y + 1) % 4, pl.ds(self.half, self.half)]
        self.far_right = self.sender.push((self.slot, 3), part, part, along(self.y, 3))

    def finish(self):
        self.far_left.wait_recv()
        self.far_right.wait_recv()


class RingReduce:
    def __init__(self, sender, slot, y, sums, part, halves, wholes):
        self.sender, self.slot, self.y, self.sums = sender, slot, y, sums
        self.part, self.halves, self.wholes = part, halves, wholes
        self.half = part.shape[1] // 2

    def send(self, k, source, target, step):
        return self.sender.push((self.slot, k), source, target, along(self.y, step))

    def begin(self):
        far, half = (self.y + 2) % 4, self.half
        self.part[far] = self.sums[far].astype(LOW)
        self.first = self.send(0, self.part.at[far, pl.ds(0, half)], self.halves.at[0], 1)
        self.second = self.send(1, self.part.at[far, pl.ds(half, half)], self.halves.at[1], 3)

    def middle(self):
        right, left, half = (self.y + 1) % 4, (self.y + 3) % 4, self.half
        self.part[right, half:] = self.sums[right, half:].astype(LOW)
        self.part[left, :half] = self.sums[left, :half].astype(LOW)
        self.first.wait_recv()
        value = self.sums[right, :half] + self.halves[0].astype(F32)
        self.part[right, :half] = value.astype(LOW)
        self.third = self.send(2, self.part.at[right], self.wholes.at[0], 1)
        self.second.wait_recv()
        value = self.sums[left, half:] + self.halves[1].astype(F32)
        self.part[left, half:] = value.astype(LOW)
        self.fourth = self.send(3, self.part.at[left], self.wholes.at[1], 3)

    def end(self):
        self.third.wait_recv()
        self.fourth.wait_recv()
        value = self.sums[self.y] + self.wholes[0].astype(F32)
        return value + self.wholes[1].astype(F32)


def ring_scratch(count, rows):
    return [
        pltpu.VMEM((count, 4, rows, D), F32),
        pltpu.VMEM((count, 4, rows, D), LOW),
        pltpu.VMEM((count, 2, rows // 2, D), LOW),
        pltpu.VMEM((count, 2, rows, D), LOW),
    ]


def fill_shuffle(shuffle):
    order = order_row()

    def body(i, carry):
        first = pl.multiple_of(i * 128, 128)
        rows = lax.broadcasted_iota(jnp.int32, (128, D), 0) + first
        shuffle[pl.ds(first, 128)] = jnp.where(rows == order, 1.0, 0.0).astype(LOW)
        return carry

    lax.fori_loop(0, 9, body, 0)


class PlaneGather:
    def __init__(self, sender, local, p, own, full, at):
        self.sender, self.local, self.p, self.own, self.full = sender, local, p, own, full
        self.at = at
        self.copies = {}

    def spot(self, h):
        z, x, c, y = self.at
        return (z, x) if h == 0 else (x, z)

    def send(self, h, k, source, target, ds, df, other=False):
        self.copies[h, k] = self.sender.push(
            (self.p, h, k), source, target, neighbour(h, *self.at, ds, df, other)
        )

    def start(self):
        c = self.at[2]
        for h in range(2):
            s, f = self.spot(h)
            mine = self.full.at[h, c, s, f]
            self.send(h, 0, self.own.at[h], mine, 0, 1)
            self.send(h, 1, self.own.at[h], mine, 0, -1)
            keep = pltpu.make_async_copy(self.own.at[h], mine, self.local.at[self.p, h])
            keep.start()
            self.copies[h, "own"] = keep

    def forward(self):
        c = self.at[2]
        width = self.own.shape[-1]
        cut = split(width)
        for h in range(2):
            s, f = self.spot(h)
            for k, df, lanes in ((0, -1, pl.ds(0, cut)), (1, 1, pl.ds(cut, width - cut))):
                self.copies[h, k].wait_recv()
                block = self.full.at[h, c, s, (f + df) % 4, :, lanes]
                self.send(h, k + 2, block, block, 0, -df)

    def start_slabs(self):
        c = self.at[2]
        for h in range(2):
            s, f = self.spot(h)
            self.copies[h, "own"].wait()
            self.copies[h, 2].wait_recv()
            self.copies[h, 3].wait_recv()
            slab = self.full.at[h, c, s]
            self.send(h, 4, slab, slab, 1, 0)
            self.send(h, 5, slab, slab, -1, 0)
            self.send(h, 8, slab, slab, 0, 0, True)

    def forward_slabs(self):
        c = self.at[2]
        for h in range(2):
            s, f = self.spot(h)
            for k, ds, first in ((4, -1, 0), (5, 1, 2)):
                self.copies[h, k].wait_recv()
                slab = self.full.at[h, c, (s + ds) % 4]
                part = self.full.at[h, c, (s + ds) % 4, pl.ds(first, 2)]
                self.send(h, k + 2, part, part, -ds, 0)
                self.send(h, k + 5, slab, slab, 0, 0, True)

    def last_slabs(self):
        c = self.at[2]
        for h in range(2):
            s, f = self.spot(h)
            self.copies[h, 6].wait_recv()
            self.copies[h, 7].wait_recv()
            slab = self.full.at[h, c, (s + 2) % 4]
            self.send(h, 11, slab, slab, 0, 0, True)

    def finish(self):
        for h in range(2):
            for k in (8, 9, 10, 11):
                self.copies[h, k].wait_recv()


class PlaneReduce:
    def __init__(self, sender, p, source, mine, buffers, out, at):
        self.sender, self.p, self.source, self.mine = sender, p, source, mine
        self.other, self.half_slab, self.whole_slab, self.half_block, self.whole_block = buffers
        self.out, self.at, self.copies = out, at, {}
        self.keep = None

    def spot(self, h):
        z, x, c, y = self.at
        return (z, x) if h == 0 else (x, z)

    def send(self, h, k, source, target, ds, df, other=False):
        self.copies[h, k] = self.sender.push(
            (self.p, h, k), source, target, neighbour(h, *self.at, ds, df, other)
        )

    def swap(self, local=None):
        c = self.at[2]
        if local is not None:
            self.keep = []
            for h in range(2):
                copy = pltpu.make_async_copy(
                    self.source(h, c), self.mine(h), local.at[self.p, h]
                )
                copy.start()
                self.keep.append(copy)
        for k, ds in ((0, 2), (9, 1), (10, -1), (11, 0)):
            for h in range(2):
                to = (self.spot(h)[0] + ds) % 4
                slab = self.source(h, 1 - c).at[to]
                self.send(h, k, slab, self.other.at[h, to], 0, 0, True)

    def slabs_far(self):
        for h in range(2):
            s, f = self.spot(h)
            mine = self.mine(h)
            if self.keep is not None:
                self.keep[h].wait()
            self.copies[h, 0].wait_recv()
            far = (s + 2) % 4

            def both(b, carry, h=h, mine=mine, far=far):
                total = mine[far, b].astype(F32) + self.other[h, far, b].astype(F32)
                mine[far, b] = total.astype(LOW)
                return carry

            lax.fori_loop(0, 4, both, 0)
            self.send(h, 1, mine.at[far, pl.ds(0, 2)], self.half_slab.at[h, 0], 1, 0)
            self.send(h, 2, mine.at[far, pl.ds(2, 2)], self.half_slab.at[h, 1], -1, 0)

    def slabs_near(self):
        for h in range(2):
            s, f = self.spot(h)
            mine = self.mine(h)
            for k, ds, first in ((1, 1, 0), (2, -1, 2)):
                self.copies[h, k + 8].wait_recv()
                self.copies[h, k].wait_recv()
                to = (s + ds) % 4
                for b in range(4):
                    total = mine[to, b].astype(F32) + self.other[h, to, b].astype(F32)
                    if first <= b < first + 2:
                        total = total + self.half_slab[h, k - 1, b - first].astype(F32)
                    mine[to, b] = total.astype(LOW)
                self.send(h, k + 2, mine.at[to], self.whole_slab.at[h, k - 1], ds, 0)

    def blocks_far(self):
        width = self.out.shape[-1]
        cut = split(width)
        for h in range(2):
            s, f = self.spot(h)
            mine = self.mine(h)
            self.copies[h, 11].wait_recv()
            self.copies[h, 3].wait_recv()
            self.copies[h, 4].wait_recv()

            def three(b, carry, h=h, s=s, mine=mine):
                total = mine[s, b].astype(F32) + self.other[h, s, b].astype(F32)
                total = total + self.whole_slab[h, 0, b].astype(F32)
                mine[s, b] = (total + self.whole_slab[h, 1, b].astype(F32)).astype(LOW)
                return carry

            lax.fori_loop(0, 4, three, 0)
            far = (f + 2) % 4
            self.send(
                h,
                5,
                mine.at[s, far, :, pl.ds(0, cut)],
                self.half_block.at[h, 0],
                0,
                1,
            )
            self.send(
                h,
                6,
                mine.at[s, far, :, pl.ds(cut, width - cut)],
                self.half_block.at[h, 1, :, pl.ds(0, width - cut)],
                0,
                -1,
            )

    def blocks_near(self):
        width = self.out.shape[-1]
        cut = split(width)
        for h in range(2):
            s, f = self.spot(h)
            mine = self.mine(h)
            for k, df, first, size in ((5, 1, 0, cut), (6, -1, cut, width - cut)):
                self.copies[h, k].wait_recv()
                to = (f + df) % 4
                lanes = slice(first, first + size)
                mine[s, to, :, lanes] = (
                    mine[s, to, :, lanes].astype(F32)
                    + self.half_block[h, k - 5, :, :size].astype(F32)
                ).astype(LOW)
                self.send(h, k + 2, mine.at[s, to], self.whole_block.at[h, k - 5], 0, df)

    def finish(self):
        for h in range(2):
            s, f = self.spot(h)
            self.copies[h, 7].wait_recv()
            self.copies[h, 8].wait_recv()
            total = self.mine(h)[s, f].astype(F32) + self.whole_block[h, 0].astype(F32)
            self.out[h] = total + self.whole_block[h, 1].astype(F32)


class RestGather(PlaneGather):
    def __init__(self, sender, p, own, near, full, at):
        super().__init__(sender, None, p, own, full, at)
        self.near = near
        self.cut = split(own.shape[-1])
        self.lanes = (pl.ds(0, self.cut), pl.ds(self.cut, own.shape[-1] - self.cut))

    def start(self):
        x = self.at[1]
        self.near[x] = self.own[...]
        self.send(0, 0, self.own, self.near.at[x], 0, 1)
        self.send(0, 1, self.own, self.near.at[x], 0, -1)

    def forward(self):
        x = self.at[1]
        for k, df in ((0, -1), (1, 1)):
            self.copies[0, k].wait_recv()
            block = self.near.at[(x + df) % 4, :, self.lanes[k]]
            self.send(0, k + 2, block, block, 0, -df)

    def start_slabs(self):
        z, x, c, y = self.at
        self.copies[0, 2].wait_recv()
        self.copies[0, 3].wait_recv()
        self.full[c, z] = self.near[...].reshape(16, self.near.shape[-1])
        slab = self.full.at[c, z]
        self.send(0, 4, slab, slab, 1, 0)
        self.send(0, 5, slab, slab, -1, 0)
        self.send(0, 8, slab, slab, 0, 0, True)

    def forward_slabs(self):
        z, x, c, y = self.at
        for k, ds in ((4, -1), (5, 1)):
            self.copies[0, k].wait_recv()
            slab = self.full.at[c, (z + ds) % 4]
            part = self.full.at[c, (z + ds) % 4, :, self.lanes[k - 4]]
            self.send(0, k + 2, part, part, -ds, 0)
            self.send(0, k + 5, slab, slab, 0, 0, True)

    def last_slabs(self):
        z, x, c, y = self.at
        self.copies[0, 6].wait_recv()
        self.copies[0, 7].wait_recv()
        slab = self.full.at[c, (z + 2) % 4]
        self.send(0, 11, slab, slab, 0, 0, True)

    def finish(self):
        for k in (8, 9, 10, 11):
            self.copies[0, k].wait_recv()


class RestReduce:
    def __init__(self, sender, p, source, mine, buffers, out, at):
        self.sender, self.p, self.source, self.mine = sender, p, source, mine
        self.other, self.half_slab, self.whole_slab = buffers[:3]
        self.blocks, self.half_block, self.whole_block = buffers[3:]
        self.out, self.at, self.copies = out, at, {}
        self.keep = None
        width = out.shape[-1]
        cut = split(width)
        self.cuts = ((0, cut), (cut, width - cut))

    def send(self, k, source, target, ds, df, other=False):
        self.copies[k] = self.sender.push(
            (self.p, 0, k), source, target, neighbour(0, *self.at, ds, df, other)
        )

    def swap(self, local=None):
        c = self.at[2]
        self.send(0, self.source.at[1 - c], self.other, 0, 0, True)
        if local is not None:
            self.keep = pltpu.make_async_copy(
                self.source.at[c], self.mine, local.at[self.p, 0]
            )
            self.keep.start()

    def slabs_far(self):
        z = self.at[0]
        if self.keep is not None:
            self.keep.wait()
        self.copies[0].wait_recv()
        for s in range(4):
            self.mine[s] = (self.mine[s].astype(F32) + self.other[s].astype(F32)).astype(LOW)
        far = (z + 2) % 4
        for i, (first, size) in enumerate(self.cuts):
            self.send(
                1 + i,
                self.mine.at[far, :, pl.ds(first, size)],
                self.half_slab.at[i, :, pl.ds(0, size)],
                (1, -1)[i],
                0,
            )

    def slabs_near(self):
        z = self.at[0]
        for i, (first, size) in enumerate(self.cuts):
            self.copies[1 + i].wait_recv()
            ds = (1, -1)[i]
            to = (z + ds) % 4
            lanes = slice(first, first + size)
            self.mine[to, :, lanes] = (
                self.mine[to, :, lanes].astype(F32) + self.half_slab[i, :, :size].astype(F32)
            ).astype(LOW)
            self.send(3 + i, self.mine.at[to], self.whole_slab.at[i], ds, 0)

    def blocks_far(self):
        z, x, c, y = self.at
        self.copies[3].wait_recv()
        self.copies[4].wait_recv()
        total = self.mine[z].astype(F32) + self.whole_slab[0].astype(F32)
        total = (total + self.whole_slab[1].astype(F32)).astype(LOW)
        self.blocks[...] = total.reshape(self.blocks.shape)
        far = (x + 2) % 4
        for i, (first, size) in enumerate(self.cuts):
            self.send(
                5 + i,
                self.blocks.at[far, :, pl.ds(first, size)],
                self.half_block.at[i, :, pl.ds(0, size)],
                0,
                (1, -1)[i],
            )

    def blocks_near(self):
        x = self.at[1]
        for i, (first, size) in enumerate(self.cuts):
            self.copies[5 + i].wait_recv()
            df = (1, -1)[i]
            to = (x + df) % 4
            lanes = slice(first, first + size)
            self.blocks[to, :, lanes] = (
                self.blocks[to, :, lanes].astype(F32) + self.half_block[i, :, :size].astype(F32)
            ).astype(LOW)
            self.send(7 + i, self.blocks.at[to], self.whole_block.at[i], 0, df)

    def finish(self):
        x = self.at[1]
        self.copies[7].wait_recv()
        self.copies[8].wait_recv()
        total = self.blocks[x].astype(F32) + self.whole_block[0].astype(F32)
        self.out[...] = total + self.whole_block[1].astype(F32)


def forward_kernel(
    query, keyvalue, output, gate, up, down_t, own_gains, tokens_in, cotangent, doc_row,
    w12, w12r, gains, attention, middle, ffn_full, upstream, *refs
):
    count = len(SAVED)
    saved, kept = refs[:count], refs[count : 2 * count]
    (
        w0, w0r, normed, query_raw, key_raw, query_rot, key_rot, value_low, probs, heads,
        x_full, cosine, sine,
    ) = kept
    (
        own0, own12, own0r, own12r, shuffle, near0, near12, ids, sums, part, halves, wholes,
        send, recv, local, ring_send, ring_recv, save_sem,
    ) = refs[2 * count :]
    z, x, c, y = at = place()
    entered = greet(z, x, c, y, True, True)
    planes = Sender(send, recv)
    rings = Sender(ring_send, ring_recv)
    qkvo = PlaneGather(planes, local, QKVO, own0, w0, at)
    ffn = PlaneGather(planes, local, FFN, own12, w12, at)
    qkvo_rest = RestGather(planes, QKVO_REST, own0r, near0, w0r, at)
    ffn_rest = RestGather(planes, FFN_REST, own12r, near12, w12r, at)
    columns = gate.shape[1]
    for h in range(2):
        rows = slice(16 * h, 16 * h + 16)
        own0[h, :, 0:256] = query[rows].astype(LOW)
        own0[h, :, 256:768] = keyvalue[rows].astype(LOW)
        own0[h, :, 768:1024] = output[rows].astype(LOW)
    own0r[:, 0:256] = query[32:36].astype(LOW)
    own0r[:, 256:768] = keyvalue[32:36].astype(LOW)
    own0r[:, 768:1024] = output[32:36].astype(LOW)
    own0r[:, 1024:1152] = jnp.zeros((4, 128), LOW)
    own0r[0:1, 1024:1152] = own_gains[:, 0:128].astype(LOW)
    own0r[1:2, 1024:1056] = own_gains[:, 128:160].astype(LOW)
    entered()
    qkvo.start()
    qkvo_rest.start()
    for first, matrix in ((0, gate), (FP, up), (2 * FP, down_t)):
        for h in range(2):
            own12[h, :, first : first + columns] = matrix[16 * h : 16 * h + 16].astype(LOW)
            own12[h, :, first + columns : first + FP] = jnp.zeros((16, FP - columns), LOW)
        own12r[:, first : first + columns] = matrix[32:36].astype(LOW)
        own12r[:, first + columns : first + FP] = jnp.zeros((4, FP - columns), LOW)
    qkvo_rest.forward()
    qkvo.forward()
    qkvo_rest.start_slabs()
    qkvo.start_slabs()
    ffn.start()
    ffn_rest.start()
    fill_shuffle(shuffle)
    x_full[y] = nn(tokens_in[...], shuffle[...]).astype(LOW)
    token_ring = RingGather(rings, 0, y, x_full)
    token_ring.start()
    qkvo_rest.forward_slabs()
    qkvo.forward_slabs()
    ffn_rest.forward()
    ffn.forward()
    ffn_rest.start_slabs()
    ffn.start_slabs()
    ids[...] = jnp.broadcast_to(doc_row[...].astype(F32), (128, 512)).T
    live = ids[pl.ds(pl.multiple_of(y * 128, 128), 128), 0:1] >= 0
    upstream[...] = jnp.where(live, nn(cotangent[...], shuffle[...]), 0.0)
    token_ring.forward()
    key_place = lax.broadcasted_iota(jnp.int32, (512, 512), 1).astype(F32)
    starts = jnp.min(
        jnp.where(ids[:, 0:1] == doc_row[...].astype(F32), key_place, 512.0),
        axis=1,
        keepdims=True,
    )
    position = lax.broadcasted_iota(jnp.int32, (512, 1), 0).astype(F32) - starts
    exponent = lax.broadcasted_iota(jnp.int32, (1, HD // 2), 1).astype(F32) * (2.0 / HD)
    angle = position * jnp.exp(exponent * -np.log(rope_base))
    cosine[...] = jnp.cos(angle)
    sine[...] = jnp.sin(angle)
    qkvo_rest.last_slabs()
    qkvo.last_slabs()
    token_ring.finish()
    qkvo_rest.finish()
    held = w0r[:, :, :, 1024:1152].reshape(128, 128)
    rows = lax.broadcasted_iota(jnp.int32, (128, D), 0)
    order = order_row()
    for n in range(5):
        holder, entry = gain_row(n, order)
        pick = jnp.where(rows == entry, 1.0, 0.0).astype(LOW)
        gains[n : n + 1] = jnp.sum(
            jnp.where(rows == holder, nn(held, pick), 0.0), axis=0, keepdims=True
        )
    gains[5:8] = jnp.zeros((3, D), F32)

    def norm_rows(t, carry):
        u = x_full[t].astype(F32)
        normed[t] = (u * rms_scale(u) * gains[0:1]).astype(LOW)
        return carry

    lax.fori_loop(0, 4, norm_rows, 0)
    qkvo.finish()
    weights = w0[:, :, :, :, :, 0:768].reshape(1024, 768)
    rest = w0r[:, :, :, 0:768].reshape(128, 768)
    whole = normed[...].reshape(512, D)
    raw = nn(whole[:, :1024], weights) + nn(whole[:, 1024:], rest)
    query_raw[...] = raw[:, :HD]
    key_raw[...] = raw[:, HD : 2 * HD]
    value_low[...] = raw[:, 2 * HD :].astype(LOW)
    cos, sin = cosine[...], sine[...]
    u = query_raw[...]
    query_rot[...] = turn(u * rms_scale(u) * gains[4:5, :HD], cos, sin).astype(LOW)
    u = key_raw[...]
    key_rot[...] = turn(u * rms_scale(u) * gains[4:5, HD : 2 * HD], cos, sin).astype(LOW)
    scores = nt(query_rot[...], key_rot[...]) * HD ** (-0.5)
    row_index = lax.broadcasted_iota(jnp.int32, (512, 512), 0)
    key_index = lax.broadcasted_iota(jnp.int32, (512, 512), 1)
    own_ids = ids[:, 0:1]
    same = (own_ids == doc_row[...].astype(F32)) & (own_ids >= 0) & (key_index <= row_index)
    scores = jnp.where(same | (key_index == row_index), scores, -1e30)
    exponents = jnp.exp(scores - jnp.max(scores, axis=-1, keepdims=True))
    probs[...] = exponents / jnp.sum(exponents, axis=-1, keepdims=True)
    heads[...] = nn(probs[...].astype(LOW), value_low[...]).astype(LOW).reshape(4, 128, HD)

    saves = [
        pltpu.make_async_copy(source, target, save_sem.at[i])
        for i, (source, target) in enumerate(zip(kept, saved))
    ]
    for save in saves:
        save.start()
    project_main = w0[:, :, :, :, :, 768:1024].reshape(1024, HD)
    project_rest = w0r[:, :, :, 768:1024].reshape(128, HD)
    reducers = []
    for m in range(2):
        block = heads[:, 64 * m : 64 * m + 64].reshape(256, HD)
        sums[m, :, :, :1024] = nt(block, project_main).reshape(4, 64, 1024)
        sums[m, :, :, 1024:] = nt(block, project_rest).reshape(4, 64, 128)
        reducers.append(
            RingReduce(rings, 1 + m, y, sums.at[m], part.at[m], halves.at[m], wholes.at[m])
        )
        reducers[m].begin()
    ffn_rest.forward_slabs()
    reducers[0].middle()
    reducers[1].middle()
    ffn.forward_slabs()
    ffn_rings = []
    for m in range(2):
        mine = slice(64 * m, 64 * m + 64)
        total = reducers[m].end()
        attention[mine] = total
        u = x_full[y, mine].astype(F32) + total * rms_scale(total) * gains[1:2]
        middle[mine] = u
        ffn_full[m, y] = (u * rms_scale(u) * gains[2:3]).astype(LOW)
        ffn_rings.append(RingGather(rings, 3 + m, y, ffn_full.at[m]))
        ffn_rings[m].start()
    ffn_rest.last_slabs()
    ffn_rings[0].forward()
    ffn_rings[1].forward()
    ffn.last_slabs()
    ffn_rings[0].finish()
    ffn_rings[1].finish()
    ffn_rest.finish()
    ffn.finish()
    for save in saves:
        save.wait()
    planes.close()
    rings.close()


def run_forward(held):
    vmem = pl.BlockSpec(memory_space=pltpu.VMEM)
    hbm = pl.BlockSpec(memory_space=pl.ANY)
    shapes = [
        (LEAD + (WIDTHS[FFN],), LOW, hbm),
        (REST_LEAD + (WIDTHS[FFN_REST],), LOW, vmem),
        ((8, D), F32, vmem),
        ((128, D), F32, vmem),
        ((128, D), F32, vmem),
        ((2, 4, 64, D), LOW, vmem),
        ((128, D), F32, vmem),
    ]
    shapes += [(shape, kind, hbm) for shape, kind in SAVED]
    return pl.pallas_call(
        forward_kernel,
        out_shape=[jax.ShapeDtypeStruct(s, t) for s, t, _ in shapes],
        in_specs=[vmem] * len(held),
        out_specs=[m for _, _, m in shapes],
        scratch_shapes=[pltpu.VMEM(shape, kind) for shape, kind in SAVED]
        + [
            pltpu.VMEM((2, 16, WIDTHS[QKVO]), LOW),
            pltpu.VMEM((2, 16, WIDTHS[FFN]), LOW),
            pltpu.VMEM((4, WIDTHS[QKVO_REST]), LOW),
            pltpu.VMEM((4, WIDTHS[FFN_REST]), LOW),
            pltpu.VMEM((D, D), LOW),
            pltpu.VMEM((4, 4, WIDTHS[QKVO_REST]), LOW),
            pltpu.VMEM((4, 4, WIDTHS[FFN_REST]), LOW),
            pltpu.VMEM((512, 128), F32),
        ]
        + ring_scratch(2, 64)
        + [
            pltpu.SemaphoreType.DMA((4, 2, 12)),
            pltpu.SemaphoreType.DMA((4, 2, 12)),
            pltpu.SemaphoreType.DMA((4, 2)),
            pltpu.SemaphoreType.DMA((5, 4)),
            pltpu.SemaphoreType.DMA((5, 4)),
            pltpu.SemaphoreType.DMA((len(SAVED),)),
        ],
        compiler_params=pltpu.CompilerParams(
            collective_id=0, has_side_effects=True, vmem_limit_bytes=VMEM_LIMIT
        ),
        name="gather_and_attend",
    )(*held)


def feed_kernel(
    ffn_full, middle, upstream, attention, gains, w12, w12r,
    block_out, middle_grad, attention_low, gain_part, g12, rest_flat,
    weights, act, slope, hidden, gate_up_low, out_full, turned, stage, shuffle,
    sums, part, halves, wholes, load_sem, store_sem, ring_send, ring_recv,
):
    z, x, c, y = place()
    loads = []
    for i, (first, size) in enumerate(((0, 2 * FP), (2 * FP, FP))):
        lanes = pl.ds(first, size)
        for k, source, row, rows in ((0, w12, 0, 1024), (1, w12r, 1024, 128)):
            load = pltpu.make_async_copy(
                source.at[:, lanes], weights.at[pl.ds(row, rows), lanes], load_sem.at[i, k]
            )
            load.start()
            loads.append(load)
    greet(z, x, c, y, False, True)()
    rings = Sender(ring_send, ring_recv)
    outward = [
        RingReduce(rings, m, y, sums.at[m], part.at[m], halves.at[m], wholes.at[m])
        for m in range(2)
    ]
    gathers = [RingGather(rings, 2 + m, y, out_full.at[m]) for m in range(2)]
    inward = [
        RingReduce(rings, 4 + m, y, sums.at[m], part.at[2 + m], halves.at[2 + m], wholes.at[2 + m])
        for m in range(2)
    ]
    mine = [slice(0, 64), slice(64, 128)]
    loads[0].wait()
    loads[1].wait()

    def chunk(j, first=0):
        return pl.ds(pl.multiple_of(first + j * 256, 256), 256)

    def feed(m, start, stop):
        def body(j, carry):
            lanes = chunk(j)
            rows = ffn_full[m].reshape(256, D)
            gate = nn(rows, weights[:, lanes])
            up = nn(rows, weights[:, chunk(j, FP)])
            t = jnp.tanh(0.7978845608 * gate * (1.0 + 0.044715 * gate * gate))
            hidden[m, :, lanes] = (0.5 * gate * (1.0 + t) * up).astype(LOW)
            act[m, :, lanes] = gate
            slope[m, :, lanes] = up
            return carry

        lax.fori_loop(start, stop, body, 0)

    def down(m):
        sums[m] = nt(hidden[m], weights[:, 2 * FP :]).reshape(4, 64, D)
        outward[m].begin()

    def after(m):
        total = outward[m].end()
        grad, gain = rms_back(total, gains[3:4], upstream[mine[m]])
        out_full[m, y] = grad.astype(LOW)
        gathers[m].start()
        value = middle[mine[m]] + total * rms_scale(total) * gains[3:4]
        return value.astype(LOW), gain

    def slopes(m, start, stop):
        def body(j, carry):
            lanes = chunk(j)
            gate = act[m, :, lanes]
            up = slope[m, :, lanes]
            square = gate * gate
            rise = jnp.tanh(0.7978845608 * gate * (1.0 + 0.044715 * square))
            half = 0.5 * (1.0 + rise)
            bend = 0.7978845608 * (1.0 + 3.0 * 0.044715 * square)
            act[m, :, lanes] = gate * half
            slope[m, :, lanes] = up * (half + 0.5 * gate * (1.0 - rise * rise) * bend)
            return carry

        lax.fori_loop(start, stop, body, 0)

    def hidden_back(m):
        def body(j, carry):
            lanes = chunk(j)
            grad = nn(out_full[m].reshape(256, D), weights[:, chunk(j, 2 * FP)])
            gate_up_low[m, :, lanes] = (grad * slope[m, :, lanes]).astype(LOW)
            gate_up_low[m, :, chunk(j, FP)] = (grad * act[m, :, lanes]).astype(LOW)
            return carry

        lax.fori_loop(0, 7, body, 0)

    def feed_back(m):
        sums[m] = nt(gate_up_low[m], weights[:, : 2 * FP]).reshape(4, 64, D)
        inward[m].begin()

    def weight_grads(left, right, start, stop, offset):
        def body(j, carry):
            slot = j % 2
            lanes = chunk(j, offset)
            copy = pltpu.make_async_copy(
                stage.at[slot], g12.at[:, lanes], store_sem.at[slot]
            )

            @pl.when((j >= 2) | (offset == 0))
            def _():
                copy.wait()

            value = nn(turned[left], right[:, :, chunk(j)].reshape(512, 256)).astype(LOW)
            stage[slot] = value[:1024]
            rest_flat[:, lanes] = value[1024:]
            copy.start()
            return carry

        lax.fori_loop(start, stop, body, 0)

    def before(m):
        total = inward[m].end()
        grad, gain3 = rms_back(middle[mine[m]], gains[2:3], total)
        grad = upstream[mine[m]] + grad
        middle_grad[mine[m]] = grad
        grad, gain2 = rms_back(attention[mine[m]], gains[1:2], grad)
        attention_low[mine[m]] = grad.astype(LOW)
        return gain2, gain3

    feed(0, 0, 7)
    loads[2].wait()
    loads[3].wait()
    down(0)
    feed(1, 0, 3)
    outward[0].middle()
    feed(1, 3, 7)
    down(1)
    out0, gain40 = after(0)
    slopes(0, 0, 7)
    outward[1].middle()
    slopes(1, 0, 4)
    gathers[0].forward()
    slopes(1, 4, 7)
    out1, gain41 = after(1)
    gain_part[3:4] = gain40 + gain41
    gathers[0].finish()
    hidden_back(0)
    gathers[1].forward()
    feed_back(0)
    turned[0] = ffn_full[...].reshape(512, D).T
    gathers[1].finish()
    hidden_back(1)
    inward[0].middle()
    feed_back(1)
    turned[1] = out_full[...].reshape(512, D).T
    weight_grads(1, hidden, 0, 7, 2 * FP)
    inward[1].middle()
    weight_grads(0, gate_up_low, 0, 7, 0)
    fill_shuffle(shuffle)
    block_out[...] = nt(jnp.concatenate([out0, out1], axis=0), shuffle[...]).astype(LOW)
    gain20, gain30 = before(0)
    weight_grads(0, gate_up_low, 7, 14, 0)
    gain21, gain31 = before(1)
    gain_part[1:2] = gain20 + gain21
    gain_part[2:3] = gain30 + gain31
    gain_part[0:1] = jnp.zeros((1, D), F32)
    gain_part[4:8] = jnp.zeros((4, D), F32)
    for slot in range(2):
        pltpu.make_async_copy(
            stage.at[slot], g12.at[:, pl.ds(0, 256)], store_sem.at[slot]
        ).wait()
    rings.close()


def run_feed(ffn_full, middle, upstream, attention, gains, w12, w12r):
    vmem = pl.BlockSpec(memory_space=pltpu.VMEM)
    hbm = pl.BlockSpec(memory_space=pl.ANY)
    shapes = [
        ((128, D), LOW, vmem),
        ((128, D), F32, vmem),
        ((128, D), LOW, vmem),
        ((8, D), F32, vmem),
        ((1024, 3 * FP), LOW, hbm),
        ((128, 3 * FP), LOW, vmem),
    ]
    return pl.pallas_call(
        feed_kernel,
        out_shape=[jax.ShapeDtypeStruct(s, t) for s, t, _ in shapes],
        in_specs=[vmem] * 5 + [hbm] * 2,
        out_specs=[m for _, _, m in shapes],
        scratch_shapes=[
            pltpu.VMEM((D, 3 * FP), LOW),
            pltpu.VMEM((2, 256, FP), F32),
            pltpu.VMEM((2, 256, FP), F32),
            pltpu.VMEM((2, 256, FP), LOW),
            pltpu.VMEM((2, 256, 2 * FP), LOW),
            pltpu.VMEM((2, 4, 64, D), LOW),
            pltpu.VMEM((2, D, 512), LOW),
            pltpu.VMEM((2, 1024, 256), LOW),
            pltpu.VMEM((D, D), LOW),
            pltpu.VMEM((2, 4, 64, D), F32),
            pltpu.VMEM((4, 4, 64, D), LOW),
            pltpu.VMEM((4, 2, 32, D), LOW),
            pltpu.VMEM((4, 2, 64, D), LOW),
            pltpu.SemaphoreType.DMA((2, 2)),
            pltpu.SemaphoreType.DMA((2,)),
            pltpu.SemaphoreType.DMA((6, 4)),
            pltpu.SemaphoreType.DMA((6, 4)),
        ],
        compiler_params=pltpu.CompilerParams(
            collective_id=1, has_side_effects=True, vmem_limit_bytes=VMEM_LIMIT
        ),
        name="feed_forward_and_back",
    )(
        ffn_full,
        middle,
        upstream,
        attention,
        gains,
        w12.reshape(1024, 3 * FP),
        w12r.reshape(128, 3 * FP),
    )


def backward_kernel(*refs):
    attention_low, middle_grad, gains, gain_part, g12, g12r = refs[:6]
    count = len(SAVED)
    saved = refs[6 : 6 + count]
    refs = refs[6 + count :]
    token_grad, out0, out0r, out_g, out12r, out_d, kv_sum, rest_sum = refs[:8]
    kept, refs = refs[8 : 8 + count], refs[8 + count :]
    (
        w0, w0r, normed, query_raw, key_raw, query_rot, key_rot, value_low, probs, heads,
        x_full, cosine, sine,
    ) = kept
    part0, part0r, mine_g, mine12r, mine_d = refs[:5]
    buffers = [refs[5:10], refs[10:15], refs[15:21], refs[21:27], refs[27:32]]
    (
        shuffle, a_full, qkv_low, turned, sums, part, halves, wholes, kv_all, rest_all,
        send, recv, local, ring_send, ring_recv, last_send, last_recv, load_sem,
    ) = refs[32:]
    z, x, c, y = at = place()
    loads = [
        pltpu.make_async_copy(source, target, load_sem.at[i])
        for i, (source, target) in enumerate(zip(saved, kept))
    ]
    for load in loads:
        load.start()
    greet(z, x, c, y, True, True, True)()
    planes = Sender(send, recv)
    rings = Sender(ring_send, ring_recv)
    lasts = Sender(last_send, last_recv)
    qkvo = PlaneReduce(
        planes,
        QKVO,
        lambda h, core: part0.at[h, core],
        lambda h: part0.at[h, c],
        buffers[QKVO],
        out0,
        at,
    )
    gate_up = PlaneReduce(
        planes,
        GATE_UP,
        lambda h, core: g12.at[h, core, :, :, :, pl.ds(0, 2 * FP)],
        lambda h: mine_g.at[h],
        buffers[GATE_UP],
        out_g,
        at,
    )
    down = PlaneReduce(
        planes,
        DOWN,
        lambda h, core: g12.at[h, core, :, :, :, pl.ds(2 * FP, FP)],
        lambda h: mine_d.at[h],
        buffers[DOWN],
        out_d,
        at,
    )
    qkvo_rest = RestReduce(
        planes, QKVO_REST, part0r, part0r.at[c], buffers[QKVO_REST], out0r, at
    )
    ffn_rest = RestReduce(planes, FFN_REST, g12r, mine12r, buffers[FFN_REST], out12r, at)
    a_full[y] = attention_low[...]
    ring = RingGather(rings, 0, y, a_full)
    ring.start()
    down.swap(local)
    ffn_rest.swap(local)
    gate_up.swap(local)
    fill_shuffle(shuffle)
    loads[2].wait()
    turned[0] = normed[...].reshape(512, D).T
    down.slabs_far()
    ring.forward()
    gate_up.slabs_far()
    for i, load in enumerate(loads):
        if i != 2:
            load.wait()
    ring.finish()
    whole = a_full[...].reshape(512, D)
    heads_low = nn(whole[:, :1024], w0[:, :, :, :, :, 768:1024].reshape(1024, HD))
    heads_low = heads_low + nn(
        whole[:, 1024:], w0r[:, :, :, 768:1024].reshape(128, HD)
    )
    heads_low = heads_low.astype(LOW)
    down.slabs_near()
    ffn_rest.slabs_far()
    p = probs[...]
    probs_grad = nt(heads_low, value_low[...])
    score = p * (probs_grad - jnp.sum(p * probs_grad, axis=-1, keepdims=True))
    score_low = score.astype(LOW)
    scale = HD ** (-0.5)
    cos, sin = cosine[...], -sine[...]
    query_grad = turn(nn(score_low, key_rot[...]) * scale, cos, sin)
    key_grad = turn(nn(score_low.T, query_rot[...]) * scale, cos, sin)
    value_grad = nn(p.astype(LOW).T, heads_low)
    gate_up.slabs_near()
    query_grad, query_gain = rms_back(query_raw[...], gains[4:5, :HD], query_grad)
    key_grad, key_gain = rms_back(key_raw[...], gains[4:5, HD : 2 * HD], key_grad)
    qkv_low[:, :, :HD] = query_grad.astype(LOW).reshape(4, 128, HD)
    qkv_low[:, :, HD : 2 * HD] = key_grad.astype(LOW).reshape(4, 128, HD)
    qkv_low[:, :, 2 * HD :] = value_grad.astype(LOW).reshape(4, 128, HD)
    down.blocks_far()
    ffn_rest.slabs_near()
    block = qkv_low[...].reshape(512, 768)
    main = nt(block, w0[:, :, :, :, :, 0:768].reshape(1024, 768))
    sums[:, :, :1024] = main.reshape(4, 128, 1024)
    rest = nt(block, w0r[:, :, :, 0:768].reshape(128, 768))
    sums[:, :, 1024:] = rest.reshape(4, 128, 128)
    reducer = RingReduce(rings, 1, y, sums, part, halves, wholes)
    reducer.begin()
    down.blocks_near()
    turned[1] = a_full[...].reshape(512, D).T
    for j in range(4):
        lanes = slice(j * 256, j * 256 + 256)
        if j < 3:
            value = nn(turned[0], qkv_low[:, :, lanes].reshape(512, 256))
        else:
            value = nn(turned[1], heads[...].reshape(512, 256))
        value = value.astype(LOW)
        part0[:, :, :, :, :, lanes] = value[:1024].reshape(LEAD + (256,))
        part0r[:, :, :, lanes] = value[1024:].reshape(REST_LEAD + (256,))
    qkvo.swap()
    reducer.middle()

    def first_gain(t, carry):
        u = x_full[t].astype(F32)
        return carry + jnp.sum(sums[t] * (u * rms_scale(u)), axis=0, keepdims=True)

    gain = lax.fori_loop(0, 4, first_gain, jnp.zeros((1, D), F32))
    rows = lax.broadcasted_iota(jnp.int32, (128, D), 0)
    order = order_row()
    shares = jnp.zeros((128, 128), F32)
    wide = [gain, gain_part[1:2], gain_part[2:3], gain_part[3:4]]
    wide.append(jnp.concatenate([query_gain, key_gain, jnp.zeros((1, D - 2 * HD), F32)], axis=1))
    for n in range(5):
        holder, entry = gain_row(n, order)
        pick = jnp.where(rows == entry, 1.0, 0.0).astype(LOW)
        placed = jnp.where(rows == holder, wide[n], 0.0).astype(LOW)
        shares = shares + nt(placed, pick)
    part0r[:, :, :, 1024:1152] = shares.astype(LOW).reshape(REST_LEAD + (128,))
    qkvo_rest.swap()
    qkvo.slabs_far()
    ffn_rest.blocks_far()
    qkvo_rest.slabs_far()
    gate_up.blocks_far()
    qkvo.slabs_near()
    qkvo_rest.slabs_near()
    total = reducer.end()
    u = x_full[y].astype(F32)
    grad, gain = rms_back(u, gains[0:1], total)
    grad = (middle_grad[...] + grad).astype(LOW)
    ffn_rest.blocks_near()
    gate_up.blocks_near()
    qkvo.blocks_far()
    qkvo_rest.blocks_far()
    token_grad[...] = nt(grad, shuffle[...]).astype(LOW)
    down.finish()
    qkvo.blocks_near()
    qkvo_rest.blocks_near()
    ffn_rest.finish()
    gate_up.finish()
    qkvo.finish()
    kv_all[y] = out0[:, :, HD : 3 * HD]
    last = []
    for step in (1, 2, 3):
        block = kv_all.at[y]
        last.append(lasts.push((0, step - 1), block, block, along(y, step)))
    qkvo_rest.finish()
    rest_all[y] = out0r[...]
    for step in (1, 2, 3):
        block = rest_all.at[y]
        last.append(lasts.push((1, step - 1), block, block, along(y, step)))
    for copy in last:
        copy.wait_recv()
    kv_sum[...] = kv_all[0] + kv_all[1] + kv_all[2] + kv_all[3]
    rest_sum[...] = rest_all[0] + rest_all[1] + rest_all[2] + rest_all[3]
    planes.close()
    rings.close()
    lasts.close()


def run_backward(held, weight_parts):
    vmem = pl.BlockSpec(memory_space=pltpu.VMEM)
    hbm = pl.BlockSpec(memory_space=pl.ANY)
    shapes = [
        ((128, D), LOW),
        ((2, 16, WIDTHS[QKVO]), F32),
        ((4, WIDTHS[QKVO_REST]), F32),
        ((2, 16, 2 * FP), F32),
        ((4, WIDTHS[FFN_REST]), F32),
        ((2, 16, FP), F32),
        ((2, 16, 2 * HD), F32),
        ((4, WIDTHS[QKVO_REST]), F32),
    ]
    def plane_scratch(width):
        return [
            pltpu.VMEM((2, 4, 4, 16, width), LOW),
            pltpu.VMEM((2, 2, 2, 16, width), LOW),
            pltpu.VMEM((2, 2, 4, 16, width), LOW),
            pltpu.VMEM((2, 2, 16, split(width)), LOW),
            pltpu.VMEM((2, 2, 16, width), LOW),
        ]

    scratch = [pltpu.VMEM(shape, kind) for shape, kind in SAVED]
    scratch += [
        pltpu.VMEM(LEAD + (WIDTHS[QKVO],), LOW),
        pltpu.VMEM(REST_LEAD + (WIDTHS[QKVO_REST],), LOW),
        pltpu.VMEM((2, 4, 4, 16, 2 * FP), LOW),
        pltpu.VMEM((4, 16, WIDTHS[FFN_REST]), LOW),
        pltpu.VMEM((2, 4, 4, 16, FP), LOW),
    ]
    scratch += plane_scratch(WIDTHS[QKVO]) + plane_scratch(2 * FP)
    for p in (QKVO_REST, FFN_REST):
        scratch += [
            pltpu.VMEM((4, 16, WIDTHS[p]), LOW),
            pltpu.VMEM((2, 16, split(WIDTHS[p])), LOW),
            pltpu.VMEM((2, 16, WIDTHS[p]), LOW),
            pltpu.VMEM((4, 4, WIDTHS[p]), LOW),
            pltpu.VMEM((2, 4, split(WIDTHS[p])), LOW),
            pltpu.VMEM((2, 4, WIDTHS[p]), LOW),
        ]
    scratch += plane_scratch(FP)
    scratch += [
        pltpu.VMEM((D, D), LOW),
        pltpu.VMEM((4, 128, D), LOW),
        pltpu.VMEM((4, 128, 3 * HD), LOW),
        pltpu.VMEM((2, D, 512), LOW),
        pltpu.VMEM((4, 128, D), F32),
        pltpu.VMEM((4, 128, D), LOW),
        pltpu.VMEM((2, 64, D), LOW),
        pltpu.VMEM((2, 128, D), LOW),
        pltpu.VMEM((4, 2, 16, 2 * HD), F32),
        pltpu.VMEM((4, 4, WIDTHS[QKVO_REST]), F32),
        pltpu.SemaphoreType.DMA((5, 2, 12)),
        pltpu.SemaphoreType.DMA((5, 2, 12)),
        pltpu.SemaphoreType.DMA((5, 2)),
        pltpu.SemaphoreType.DMA((2, 4)),
        pltpu.SemaphoreType.DMA((2, 4)),
        pltpu.SemaphoreType.DMA((2, 3)),
        pltpu.SemaphoreType.DMA((2, 3)),
        pltpu.SemaphoreType.DMA((len(SAVED),)),
    ]
    return pl.pallas_call(
        backward_kernel,
        out_shape=[jax.ShapeDtypeStruct(s, t) for s, t in shapes],
        in_specs=[vmem] * len(held) + [hbm] * len(weight_parts),
        out_specs=[vmem] * len(shapes),
        scratch_shapes=scratch,
        compiler_params=pltpu.CompilerParams(
            collective_id=2, has_side_effects=True, vmem_limit_bytes=VMEM_LIMIT
        ),
        name="attend_back_and_reduce",
    )(*held, *weight_parts)


def adam_kernel(*refs):
    out0, out0r, out_g, out12r, out_d, kv_sum, rest_sum, block_in, token_in = refs[:9]
    state, results = refs[9:30], refs[30:]
    results[0][...] = block_in[...]
    results[1][...] = token_in[...]
    columns = state[9].shape[1]
    places = (
        (out0, out0r, 0, 0, HD, D),
        (kv_sum, rest_sum, 0, HD, 2 * HD, D),
        (out0, out0r, 3 * HD, 3 * HD, HD, H * HD),
        (out_g, out12r, 0, 0, columns, D),
        (out_g, out12r, FP, FP, columns, D),
        (out_d, out12r, 0, 2 * FP, columns, FF),
    )
    for i, (main, rest, first, rest_first, width, fan_in) in enumerate(places):
        weight, moment, second = state[3 * i : 3 * i + 3]
        for h in range(3):
            rows = slice(16 * h, min(16 * h + 16, 36))
            if h < 2:
                gradient = main[h, :, first : first + width]
            else:
                gradient = rest[:, rest_first : rest_first + width]
            updated = adam_update(
                weight[rows],
                gradient,
                moment[rows],
                second[rows],
                matrix_rate * fan_in ** (-0.5),
                weight_decay,
            )
            for k in range(3):
                results[2 + 3 * i + k][rows] = updated[k]
    gradient = jnp.concatenate([rest_sum[0:1, 1024:1152], rest_sum[1:2, 1024:1056]], axis=1)
    updated = adam_update(
        state[18][...], gradient, state[19][...], state[20][...], gain_rate, 0.0
    )
    for k in range(3):
        results[20 + k][...] = updated[k]


def run_adam(gradients, tokens, state):
    shapes = [(v.shape, v.dtype) for v in tokens]
    for i in range(0, len(state), 3):
        shapes += [(state[i].shape, F32)] * 3
    return pl.pallas_call(
        adam_kernel,
        out_shape=[jax.ShapeDtypeStruct(shape, kind) for shape, kind in shapes],
        compiler_params=pltpu.CompilerParams(vmem_limit_bytes=VMEM_LIMIT),
        name="adam",
    )(*gradients, *tokens, *state)


def per_device(
    tokens,
    document_ids,
    cotangent,
    query_weight,
    keyvalue_weight,
    output_weight,
    gate_weight,
    up_weight,
    down_weight,
    norm_gains,
    query_first,
    query_second,
    keyvalue_first,
    keyvalue_second,
    output_first,
    output_second,
    gate_first,
    gate_second,
    up_first,
    up_second,
    down_first,
    down_second,
    gain_first,
    gain_second,
):
    w12, w12r, gains, attention, middle, ffn_full, upstream, *saved = run_forward(
        (
            query_weight, keyvalue_weight, output_weight.T, gate_weight, up_weight,
            down_weight.T, norm_gains[None, :], tokens, cotangent, document_ids[None, :],
        )
    )
    block_output, middle_grad, attention_low, gain_part, g12, g12r = run_feed(
        ffn_full, middle, upstream, attention, gains, w12, w12r
    )
    token_grad, *gradients = run_backward(
        (attention_low, middle_grad, gains, gain_part),
        (
            g12.reshape(LEAD + (WIDTHS[FFN],)),
            g12r.reshape(REST_LEAD + (WIDTHS[FFN_REST],)),
            *saved,
        ),
    )
    (
        block_output, token_grad, query_next, query_one, query_two, keyvalue_next, keyvalue_one,
        keyvalue_two, output_next, output_one, output_two, gate_next, gate_one, gate_two,
        up_next, up_one, up_two, down_next, down_one, down_two, gain_next, gain_one, gain_two,
    ) = run_adam(
        gradients,
        (block_output, token_grad),
        (
            query_weight, query_first, query_second,
            keyvalue_weight, keyvalue_first, keyvalue_second,
            output_weight.T, output_first.T, output_second.T,
            gate_weight, gate_first, gate_second,
            up_weight, up_first, up_second,
            down_weight.T, down_first.T, down_second.T,
            norm_gains[None, :], gain_first[None, :], gain_second[None, :],
        ),
    )
    return (
        block_output, token_grad, query_next, query_one, query_two, keyvalue_next, keyvalue_one,
        keyvalue_two, output_next.T, output_one.T, output_two.T, gate_next, gate_one, gate_two,
        up_next, up_one, up_two, down_next.T, down_one.T, down_two.T,
        gain_next[0], gain_one[0], gain_two[0],
    )


def solution(mesh):
    placed = (
        P(("dp", "tensor"), None),
        P("dp"),
        P(("dp", "tensor"), None),
        P("dp", "tensor"),
        P("dp", None),
        P("tensor", "dp"),
        P("dp", "tensor"),
        P("dp", "tensor"),
        P("tensor", "dp"),
        P("dp"),
        P("dp", "tensor"),
        P("dp", "tensor"),
        P("dp", None),
        P("dp", None),
        P("tensor", "dp"),
        P("tensor", "dp"),
        P("dp", "tensor"),
        P("dp", "tensor"),
        P("dp", "tensor"),
        P("dp", "tensor"),
        P("tensor", "dp"),
        P("tensor", "dp"),
        P("dp"),
        P("dp"),
    )
    return jax.shard_map(
        per_device,
        mesh=mesh,
        in_specs=placed,
        out_specs=(
            P(("dp", "tensor"), None),
            P(("dp", "tensor"), None),
            P("dp", "tensor"),
            P("dp", "tensor"),
            P("dp", "tensor"),
            P("dp", None),
            P("dp", None),
            P("dp", None),
            P("tensor", "dp"),
            P("tensor", "dp"),
            P("tensor", "dp"),
            P("dp", "tensor"),
            P("dp", "tensor"),
            P("dp", "tensor"),
            P("dp", "tensor"),
            P("dp", "tensor"),
            P("dp", "tensor"),
            P("tensor", "dp"),
            P("tensor", "dp"),
            P("tensor", "dp"),
            P("dp"),
            P("dp"),
            P("dp"),
        ),
        check_vma=False,
    )
```
